256 devices in a mesh: blk: 32 (over x, z), grp: 8 (over y, core).
Axes of the slice: x: 4, y: 4, z: 8, core: 2. Of those that a mesh axis runs over, the one named last changes fastest.
Arguments:
- features: bfloat16 [8, 8192, 256], P('grp', 'blk'), may hold values from -6 to 6
- weight: bfloat16 [256, 256], replicated, may hold values from -0.375 to 0.375
- cotangent: bfloat16 [8, 8192, 256], P('grp', 'blk'), may hold values from -6 to 6
- dense_tiles: bfloat16 [8, 32, 64, 128, 128], P('grp', 'blk'), as said below
- dense_cols: int32 [8, 32, 64], P('grp', 'blk'), may hold values from 0 to 1, as said below
- sparse_tiles: bfloat16 [8, 32, 32, 128, 128], P('grp', 'blk'), may hold values from -0.09375 to 0.09375
- sparse_rows: int32 [8, 32, 32], P('grp', 'blk'), may hold values from 0 to 1
- sparse_cols: int32 [8, 32, 32], P('grp', 'blk'), may hold values from 0 to 7
- send_rows: int32 [8, 32, 8, 128], P('grp', 'blk'), may hold values from 0 to 255
- send_counts: int32 [8, 32, 8], P('grp', 'blk'), may hold values from 16 to 128, as said below
Outputs:
- hidden: bfloat16 [8, 8192, 256], P('grp', 'blk')
- grad_features: bfloat16 [8, 8192, 256], P('grp', 'blk')
- grad_weight: float32 [256, 256], replicated
The draws below stay inside these ranges and needn't reach their ends.
Inputs may be any that keep to these rules, and one draw needn't show every extreme that they name: Tile t of device (g, b) has row tile t % 2 and source block t // 2; for one device and one source block the 2 tiles name distinct column tiles, and the adjacency given by dense_tiles and dense_cols inside each group is symmetric. `dense_tiles`: together with dense_cols the tiles give a symmetric adjacency inside each group. `send_counts`: entry [s, b, g] counts the rows that device (s, b) sends to device (g, b); for every block index some receiver gets 128 rows from every sender.
All inputs are finite; a program needn't handle non-finite values.
Results may differ from the reference program's by a relative error of at most 0.0065.
Values may be sent and summed in bfloat16 or wider, within the bound.
No kernel may reach another device: no remote copies, remote signals or barrier semaphores. Data moves between devices by JAX's collectives and lax.ppermute only.
A program may use at most 64 MiB of HBM per device.

```python
import jax
import jax.numpy as jnp
from jax import lax

F = 256
H = 256
TILE = 128
CAP = 128
ROWS = 256
SPARSE_TILES = 32
RT = 2
NVG = 8192
DT = 64
RECV_BLK = 8
NV = 65536
N_BLK = 32
N_GRP = 8


def pair_perms(key):
    scores = jax.random.randint(key, (N_GRP, N_BLK, N_BLK, RT), 0, 1 << 20) * RT + jnp.arange(RT, dtype=jnp.int32)
    forward = jnp.argsort(scores, axis=-1).astype(jnp.int32)
    inverse = jnp.argsort(forward, axis=-1).astype(jnp.int32)
    block_row = jnp.arange(N_BLK)[:, None, None]
    block_col = jnp.arange(N_BLK)[None, :, None]
    identity = jnp.broadcast_to(jnp.arange(RT, dtype=jnp.int32), forward.shape)
    return jnp.where(block_row < block_col, forward, jnp.where(block_row > block_col, jnp.swapaxes(inverse, 1, 2), identity))


def draw_dense_tiles(key, part):
    tile_cols = pair_perms(key)
    key = jax.random.fold_in(key, 11)
    scale = (2.0 * N_BLK * TILE) ** (-0.5)
    block_row = jnp.arange(N_BLK)[:, None, None, None, None]
    block_col = jnp.arange(N_BLK)[None, :, None, None, None]

    def one_group(group_index):
        group_key = jax.random.fold_in(key, group_index)
        base = jax.random.normal(group_key, (N_BLK, N_BLK, RT, TILE, TILE), jnp.float32)
        base = base * scale
        cols_here = tile_cols[group_index]
        mirror = jnp.swapaxes(base, 0, 1)
        picked = jnp.zeros_like(base)
        for source_tile in range(RT):
            picked = picked + jnp.where((cols_here == source_tile)[:, :, :, None, None], mirror[:, :, source_tile][:, :, None], 0.0)
        flipped = jnp.swapaxes(picked, -1, -2)
        symmetric = 0.5 * (base + jnp.swapaxes(base, -1, -2))
        return jnp.where(block_row < block_col, base, jnp.where(block_row > block_col, flipped, symmetric))
    values = lax.map(one_group, jnp.arange(N_GRP, dtype=jnp.int32))
    return values.reshape(N_GRP, N_BLK, N_BLK * RT, TILE, TILE).astype(jnp.bfloat16)


def draw_dense_cols(key, part):
    tile_cols = pair_perms(key)
    return tile_cols.reshape(N_GRP, N_BLK, N_BLK * RT).astype(jnp.int32)


def draw_send_counts(key, part):
    key = jax.random.fold_in(key, 23)
    base = jax.random.randint(key, (N_GRP, N_BLK, N_GRP), CAP // 8, CAP + 1)
    hottest = jax.random.randint(jax.random.fold_in(key, 1), (N_BLK,), 0, N_GRP)
    filled = jnp.arange(N_GRP)[None, None, :] == hottest[None, :, None]
    return jnp.where(filled, CAP, base).astype(jnp.int32)


def with_ends(values, own_key, low, high):
    shape = values.shape
    spot = [jax.random.randint(jax.random.fold_in(own_key, axis), (), 0, shape[axis]) for axis in range(len(shape))]
    values = values.at[tuple(spot)].set(low)
    longest = shape.index(max(shape))
    spot[longest] = (spot[longest] + 1) % shape[longest]
    return values.at[tuple(spot)].set(high)


def steps_of(own_key, shape, shards, smallest, largest):
    loudness, own = 1.0, jax.random.fold_in(own_key, 6)
    for axis_at, blocks in shards:
        steps = jnp.exp(jax.random.uniform(jax.random.fold_in(own, axis_at), (blocks,), jnp.float32, smallest / len(shards), largest / len(shards)))
        loudness = loudness * jnp.repeat(steps, shape[axis_at] // blocks).reshape([-1 if axis == axis_at else 1 for axis in range(len(shape))])
    return loudness


def bell_draw(own_key, dims, scale, reach, shards=(), kind=jnp.bfloat16):
    values = jax.random.normal(own_key, dims, jnp.float32) * scale
    if len(shards) > 0:
        values = steps_of(own_key, dims, shards, -0.22, 0.18) * values
    return jnp.clip(values, min=-reach, max=reach).astype(kind)


def setup_inputs(seed: int = 0) -> dict:
    keys = jax.random.split(jax.random.key(seed), 11)
    features = bell_draw(keys[0], (N_GRP, NVG, F), 1.0, 6.0, ((0, 8), (1, 32)))
    weight = bell_draw(keys[1], (F, H), F ** -0.5, 0.375)
    cotangent = bell_draw(keys[2], (N_GRP, NVG, H), 1.0, 6.0, ((0, 8), (1, 32)))
    dense_tiles = draw_dense_tiles(jax.random.fold_in(keys[10], 71), 0)
    dense_cols = draw_dense_cols(jax.random.fold_in(keys[10], 71), 0)
    sparse_tiles = bell_draw(keys[5], (N_GRP, N_BLK, SPARSE_TILES, TILE, TILE), (2 * SPARSE_TILES * TILE // RT) ** -0.5, 0.09375, ((0, 8), (1, 32)))
    sparse_rows = with_ends(jax.random.randint(keys[6], (N_GRP, N_BLK, SPARSE_TILES), 0, RT), jax.random.fold_in(keys[6], 1), 0, RT - 1).astype(jnp.int32)
    sparse_cols = with_ends(jax.random.randint(keys[7], (N_GRP, N_BLK, SPARSE_TILES), 0, RECV_BLK), jax.random.fold_in(keys[7], 1), 0, RECV_BLK - 1).astype(jnp.int32)
    send_rows = with_ends(jax.random.randint(keys[8], (N_GRP, N_BLK, N_GRP, CAP), 0, ROWS), jax.random.fold_in(keys[8], 1), 0, ROWS - 1).astype(jnp.int32)
    send_counts = draw_send_counts(jax.random.fold_in(keys[10], 71), 0)
    return dict(features=features, weight=weight, cotangent=cotangent, dense_tiles=dense_tiles, dense_cols=dense_cols, sparse_tiles=sparse_tiles, sparse_rows=sparse_rows, sparse_cols=sparse_cols, send_rows=send_rows, send_counts=send_counts)


def aggregate_one(device_index, projected, dense_tiles, dense_cols, sparse_tiles, sparse_rows, sparse_cols, send_rows, send_counts):
    group_index = device_index // N_BLK
    block_index = device_index % N_BLK
    tile_values = dense_tiles[group_index, block_index].astype(jnp.float32)
    source_tiles = projected[group_index].reshape(N_BLK * RT, TILE, H)
    tile_source = (jnp.arange(DT, dtype=jnp.int32) // RT) * RT + dense_cols[group_index, block_index]
    source = source_tiles[tile_source].astype(jnp.float32)
    dense_part = jnp.einsum("tij,tjh->tih", tile_values, source, precision=lax.Precision.HIGHEST)
    dense_part = dense_part.reshape(N_BLK, RT, TILE, H).sum(axis=0)
    sent_lists = send_rows[:, block_index, group_index, :]
    sent_counts = send_counts[:, block_index, group_index]
    picked = projected[jnp.arange(N_GRP, dtype=jnp.int32)[:, None], block_index * ROWS + sent_lists]
    in_use = jnp.arange(CAP, dtype=jnp.int32)[None, :] < sent_counts[:, None]
    received = jnp.where(in_use[:, :, None], picked, jnp.zeros((), jnp.bfloat16)).reshape(RECV_BLK, TILE, H)
    sparse_vals = sparse_tiles[group_index, block_index].astype(jnp.float32)
    products = jnp.einsum("uij,ujh->uih", sparse_vals, received[sparse_cols[group_index, block_index]].astype(jnp.float32), precision=lax.Precision.HIGHEST)
    row_pick = (sparse_rows[group_index, block_index][:, None] == jnp.arange(RT, dtype=jnp.int32)[None, :]).astype(jnp.float32)
    sparse_part = jnp.einsum("ur,uih->rih", row_pick, products, precision=lax.Precision.HIGHEST)
    return (dense_part + sparse_part).reshape(ROWS, H)


def dense_back_group(group_index, grad_pre, dense_tiles, dense_cols):
    def add_block(running, block_index):
        tile_values = dense_tiles[group_index, block_index].astype(jnp.float32).reshape(N_BLK, RT, TILE, TILE)
        own_rows = lax.dynamic_slice_in_dim(grad_pre[group_index], (block_index * ROWS).astype(jnp.int32), ROWS, 0)
        own_rows = own_rows.reshape(RT, TILE, H).astype(jnp.float32)
        moved = jnp.einsum("crij,rih->crjh", tile_values, own_rows, precision=lax.Precision.HIGHEST)
        target = jnp.arange(N_BLK, dtype=jnp.int32)[:, None] * RT + dense_cols[group_index, block_index].reshape(N_BLK, RT)
        running = running.at[target.reshape(-1)].add(moved.reshape(DT, TILE, H))
        return running, None

    empty_total = jnp.zeros((N_BLK * RT, TILE, H), jnp.float32)
    result, _ = lax.scan(add_block, empty_total, jnp.arange(N_BLK, dtype=jnp.int32))
    return result.reshape(NVG, H)


def slot_grads_one(device_index, grad_pre, sparse_tiles, sparse_rows, sparse_cols):
    group_index = device_index // N_BLK
    block_index = device_index % N_BLK
    own_rows = lax.dynamic_slice_in_dim(grad_pre[group_index], (block_index * ROWS).astype(jnp.int32), ROWS, 0)
    own_rows = own_rows.reshape(RT, TILE, H)
    sparse_vals = sparse_tiles[group_index, block_index].astype(jnp.float32)
    tile_grads = jnp.einsum("uij,uih->ujh", sparse_vals, own_rows[sparse_rows[group_index, block_index]].astype(jnp.float32), precision=lax.Precision.HIGHEST)
    block_pick = (sparse_cols[group_index, block_index][:, None] == jnp.arange(RECV_BLK, dtype=jnp.int32)[None, :]).astype(jnp.float32)
    slot_grad = jnp.einsum("uq,ujh->qjh", block_pick, tile_grads, precision=lax.Precision.HIGHEST)
    return slot_grad.reshape(N_GRP, CAP, H)


def reference(features, weight, cotangent, dense_tiles, dense_cols, sparse_tiles, sparse_rows, sparse_cols, send_rows, send_counts):
    projected = jnp.dot(features.reshape(N_GRP * NVG, F), weight, preferred_element_type=jnp.float32)
    projected = projected.astype(jnp.bfloat16).reshape(N_GRP, NVG, H)
    device_ids = jnp.arange(N_GRP * N_BLK, dtype=jnp.int32)
    pre_act = lax.map(lambda device_index: aggregate_one(device_index, projected, dense_tiles, dense_cols, sparse_tiles, sparse_rows, sparse_cols, send_rows, send_counts), device_ids)
    pre_act = pre_act.reshape(N_GRP, NVG, H)
    sigmoid_pre = jax.nn.sigmoid(pre_act)
    hidden = (pre_act * sigmoid_pre).astype(jnp.bfloat16)
    grad_pre = (cotangent.astype(jnp.float32) * sigmoid_pre * (1.0 + pre_act * (1.0 - sigmoid_pre))).astype(jnp.bfloat16)
    dense_back = lax.map(lambda group_index: dense_back_group(group_index, grad_pre, dense_tiles, dense_cols), jnp.arange(N_GRP, dtype=jnp.int32))
    slots_all = lax.map(lambda device_index: slot_grads_one(device_index, grad_pre, sparse_tiles, sparse_rows, sparse_cols), device_ids)
    slots_all = slots_all.reshape(N_GRP, N_BLK, N_GRP, CAP, H)
    counts_seen = jnp.transpose(send_counts, (2, 1, 0))
    in_use = jnp.arange(CAP, dtype=jnp.int32)[None, None, None, :] < counts_seen[:, :, :, None]
    slot_values = jnp.where(in_use[..., None], slots_all, 0.0)
    lists_seen = jnp.transpose(send_rows, (2, 1, 0, 3))
    sender_group = jnp.arange(N_GRP, dtype=jnp.int32)[None, None, :, None]
    sender_block = jnp.arange(N_BLK, dtype=jnp.int32)[None, :, None, None]
    target = sender_group * NVG + sender_block * ROWS + lists_seen
    sparse_back = jnp.zeros((N_GRP * NVG, H), jnp.float32).at[target.reshape(-1)].add(slot_values.reshape(-1, H))
    agg_grad = (dense_back.reshape(N_GRP * NVG, H) + sparse_back).astype(jnp.bfloat16)
    grad_features = jnp.dot(agg_grad, weight.T, preferred_element_type=jnp.float32).astype(jnp.bfloat16)
    grad_weight = jnp.dot(features.reshape(N_GRP * NVG, F).T, agg_grad, preferred_element_type=jnp.float32) * (float(NV) ** -0.5)
    return hidden, grad_features.reshape(N_GRP, NVG, F), grad_weight
```

```python
import functools

import jax
import jax.numpy as jnp
from jax import lax
from jax.experimental import pallas as pl
from jax.experimental.pallas import tpu as pltpu
from jax.sharding import PartitionSpec as P

NX, NZ = 4, 8
TILE = 128
BF = jnp.bfloat16
F32 = jnp.float32
VMEM_LIMIT = 40 * 1024 * 1024


def swap_z(kind):
    def partner(z):
        if kind == 0:
            return z ^ 1
        return (z - 1) % NZ if z % 2 == 0 else (z + 1) % NZ

    return [(x * NZ + z, x * NZ + partner(z)) for x in range(NX) for z in range(NZ)]


def swap_x(kind):
    def partner(x):
        if kind == 0:
            return x ^ 1
        return (x - 1) % NX if x % 2 == 0 else (x + 1) % NX

    return [(x * NZ + z, partner(x) * NZ + z) for x in range(NX) for z in range(NZ)]


def go_z(v, kind):
    return lax.ppermute(v, "blk", swap_z(kind))


def go_x(v, kind):
    return lax.ppermute(v, "blk", swap_x(kind))


def ring_z(v):
    out = [v]
    up, down = go_z(v, 0), go_z(v, 1)
    out += [up, down]
    for _ in range(2):
        up, down = go_z(down, 0), go_z(up, 1)
        out += [up, down]
    h = v.shape[0] // 2
    last = jnp.concatenate([go_z(down[:h], 0), go_z(up[h:], 1)])
    return out + [last]


def ring_x(v):
    up, down = go_x(v, 0), go_x(v, 1)
    h = v.shape[0] // 2
    return [v, up, down, go_x(down[:h], 0), go_x(up[h:], 1)]


def gather(v):
    first = ring_z(jnp.concatenate(ring_x(v[:TILE])))
    second = ring_x(jnp.concatenate(ring_z(v[TILE:])))
    return first + second


def dot(a, b, ca=1, cb=0):
    return lax.dot_general(a, b, (((ca,), (cb,)), ((), ())), preferred_element_type=F32)


def select_kernel(count_ref, rows_ref, x_ref, sel_ref, out_ref):
    lane = lax.broadcasted_iota(jnp.int32, (1, TILE), 1)
    row = lax.broadcasted_iota(jnp.int32, (2 * TILE, TILE), 0)
    for s in range(rows_ref.shape[0]):
        listed = jnp.where(lane < count_ref[s], rows_ref[s : s + 1, :], -1)
        sel = jnp.where(row == listed, 1.0, 0.0).astype(BF)
        sel_ref[:, s * TILE : (s + 1) * TILE] = sel
        out_ref[s] = dot(sel, x_ref[...], 0, 0).astype(BF)


def dense_kernel(place_ref, cols_ref, tiles_ref, out_ref):
    x, z = place_ref[0], place_ref[1]
    sx, sz = 1 - 2 * (x % 2), 1 - 2 * (z % 2)
    zero = jnp.zeros((TILE, TILE), BF)
    zs = [lax.rem(z + NZ + k * sz, NZ) for k in (0, 1, -1, 2, -2, 3, -3, 4)]
    xs = [lax.rem(x + NX + k * sx, NX) for k in (0, 1, -1, 2)]
    slots = [(xv, zv, 0) for zv in zs for xv in xs] + [(xv, zv, 1) for xv in xs for zv in zs]
    for i, (xv, zv, half) in enumerate(slots):
        block = xv * NZ + zv
        r = jnp.where(cols_ref[2 * block] == half, 0, 1)
        tile = tiles_ref[2 * block + r]
        cols = slice(i * TILE, (i + 1) * TILE)
        out_ref[:TILE, cols] = jnp.where(r == 0, tile, zero)
        out_ref[TILE:, cols] = jnp.where(r == 1, tile, zero)


def sparse_kernel(rows_ref, cols_ref, tiles_ref, out_ref, total):
    total[...] = jnp.zeros_like(total)
    for u in range(tiles_ref.shape[0]):
        at = rows_ref[u] * 8 + cols_ref[u]
        total[at] += tiles_ref[u].astype(F32)
    for r in range(2):
        for q in range(8):
            value = total[r * 8 + q]
            high = value.astype(BF)
            low = (value - high.astype(F32)).astype(BF)
            rows = slice(r * TILE, (r + 1) * TILE)
            out_ref[rows, q * TILE : (q + 1) * TILE] = high
            out_ref[rows, (8 + q) * TILE : (9 + q) * TILE] = low


def split(v):
    high = v.astype(BF)
    return high, (v - high.astype(F32)).astype(BF)


def dense_product(a_ref, pieces):
    total, at = None, 0
    for p in pieces:
        n = p.shape[0]
        term = dot(a_ref[:, at : at + n], p[...])
        total = term if total is None else total + term
        at += n
    return total


def forward_kernel(n, *refs):
    a_ref, s_ref, rec_ref, w_ref, cot_ref = refs[:5]
    pieces = refs[5 : 5 + n]
    hidden_ref, grad_ref, slot_ref, pw_ref = refs[5 + n :]
    half = s_ref.shape[1] // 2
    agg = dense_product(a_ref, pieces)
    agg += dot(s_ref[:, :half], rec_ref[...]) + dot(s_ref[:, half:], rec_ref[...])
    high, low = split(agg)
    pre = dot(high, w_ref[...]) + dot(low, w_ref[...])
    sig = jax.nn.sigmoid(pre)
    hidden_ref[...] = (pre * sig).astype(BF)
    grad = (cot_ref[...].astype(F32) * sig * (1.0 + pre * (1.0 - sig))).astype(BF)
    grad_ref[...] = grad
    slot_ref[...] = (dot(s_ref[:, :half], grad, 0, 0) + dot(s_ref[:, half:], grad, 0, 0)).astype(BF)
    pw_ref[...] = dot(high, grad, 0, 0) + dot(low, grad, 0, 0)


def backward_kernel(n, *refs):
    a_ref, sel_ref, ret_ref, w_ref = refs[:4]
    pieces = refs[4 : 4 + n]
    (out_ref,) = refs[4 + n :]
    agg = dense_product(a_ref, pieces) + dot(sel_ref[...], ret_ref[...])
    out_ref[...] = dot(agg.astype(BF), w_ref[...], 1, 1).astype(BF)


SMEM = pl.BlockSpec(memory_space=pltpu.SMEM)
VMEM = pl.BlockSpec(memory_space=pltpu.VMEM)


def call(kernel, ins, outs, scalars=0, scratch=(), name=None, flops=0):
    many = isinstance(outs, list)
    moved = sum(v.size * v.dtype.itemsize for v in list(ins) + (outs if many else [outs]))
    return pl.pallas_call(
        kernel,
        out_shape=outs,
        in_specs=[SMEM] * scalars + [VMEM] * (len(ins) - scalars),
        out_specs=[VMEM] * len(outs) if many else VMEM,
        scratch_shapes=list(scratch),
        compiler_params=pltpu.CompilerParams(vmem_limit_bytes=VMEM_LIMIT),
        cost_estimate=pl.CostEstimate(flops=flops, bytes_accessed=moved, transcendentals=0),
        name=name,
    )(*ins)


def body(
    features,
    weight,
    cotangent,
    dense_tiles,
    dense_cols,
    sparse_tiles,
    sparse_rows,
    sparse_cols,
    send_rows,
    send_counts,
):
    shape = jax.ShapeDtypeStruct
    own = features[0]
    blk = lax.axis_index("blk")
    place = jnp.stack([blk // NZ, blk % NZ]).astype(jnp.int32)
    sel, outgoing = call(
        select_kernel,
        [send_counts[0, 0], send_rows[0, 0], own],
        [shape((256, 1024), BF), shape((8, TILE, 256), BF)],
        scalars=1,
        name="select",
        flops=2 * 1024 * 256 * 256,
    )
    received = lax.all_to_all(outgoing, "grp", 0, 0, tiled=True).reshape(1024, 256)
    pieces = gather(own)
    dense = call(
        dense_kernel,
        [place, dense_cols[0, 0], dense_tiles[0, 0]],
        shape((256, 64 * TILE), BF),
        scalars=2,
        name="dense",
    )
    sparse = call(
        sparse_kernel,
        [sparse_rows[0, 0], sparse_cols[0, 0], sparse_tiles[0, 0]],
        shape((256, 2048), BF),
        scalars=2,
        scratch=[pltpu.VMEM((16, TILE, TILE), F32)],
        name="sparse",
    )
    hidden, grad, slots, partial = call(
        functools.partial(forward_kernel, len(pieces)),
        [dense, sparse, received, weight, cotangent[0]] + pieces,
        [shape((256, 256), BF), shape((256, 256), BF), shape((1024, 256), BF), shape((256, 256), F32)],
        name="forward",
        flops=2 * 256 * 8192 * 256,
    )
    grad_pieces = gather(grad)
    returned = lax.all_to_all(slots.reshape(8, TILE, 256), "grp", 0, 0, tiled=True).reshape(1024, 256)
    parts = lax.all_to_all(partial.reshape(8, 32, 256), "grp", 0, 0, tiled=True)
    part = jnp.sum(parts, axis=0)
    for step in (1, 2, 4, 8, 16):
        part = part + lax.ppermute(part, "blk", [(i, i ^ step) for i in range(NX * NZ)])
    part = part * float(65536) ** -0.5
    grad_weight = lax.all_to_all(jnp.broadcast_to(part[None], (8, 32, 256)), "grp", 0, 0, tiled=True)
    grad_features = call(
        functools.partial(backward_kernel, len(grad_pieces)),
        [dense, sel, returned, weight] + grad_pieces,
        shape((256, 256), BF),
        name="backward",
        flops=2 * 256 * 8192 * 256,
    )
    return hidden[None], grad_features[None], grad_weight.reshape(256, 256)


def solution(mesh):
    three, four = P("grp", "blk", None), P("grp", "blk", None, None)
    five = P("grp", "blk", None, None, None)
    return jax.shard_map(
        body,
        mesh=mesh,
        in_specs=(three, P(), three, five, three, five, three, three, four, three),
        out_specs=(three, three, P()),
        check_vma=False,
    )
```

```python
import jax
import jax.numpy as jnp
from jax import lax
from jax.experimental import pallas as pl
from jax.experimental.pallas import tpu as pltpu
from jax.sharding import PartitionSpec as P

NX, NZ = 4, 8
TILE = 128
PIECES = 12
SELECT_AT = 1
BF = jnp.bfloat16
F32 = jnp.float32
VMEM_LIMIT = 58 * 1024 * 1024


def swap_z(kind):
    def partner(z):
        if kind == 0:
            return z ^ 1
        return (z - 1) % NZ if z % 2 == 0 else (z + 1) % NZ

    return [(x * NZ + z, x * NZ + partner(z)) for x in range(NX) for z in range(NZ)]


def swap_x(kind):
    def partner(x):
        if kind == 0:
            return x ^ 1
        return (x - 1) % NX if x % 2 == 0 else (x + 1) % NX

    return [(x * NZ + z, partner(x) * NZ + z) for x in range(NX) for z in range(NZ)]


def go_z(v, kind):
    return lax.ppermute(v, "blk", swap_z(kind))


def go_x(v, kind):
    return lax.ppermute(v, "blk", swap_x(kind))


def across_z(v):
    return lax.ppermute(v, "blk", [(i, i ^ 4) for i in range(NX * NZ)])


def tie(values, *others):
    return lax.optimization_barrier((values, others))[0]


def gather(v, hook):
    u1, d1, across = go_z(v, 0), go_z(v, 1), across_z(v)
    u1, d1 = hook(0, (u1, d1))
    u2, d2 = go_z(d1, 0), go_z(u1, 1)
    p = jnp.concatenate([v, u1, d1])
    pu, pd = go_x(p, 0), go_x(p, 1)
    u2, d2 = hook(1, (u2, d2))
    u3, d3 = go_z(d2, 0), go_z(u2, 1)
    q = jnp.concatenate([u2, d2, across])
    qu, qd = go_x(q, 0), go_x(q, 1)
    u3, d3 = hook(2, (u3, d3))
    r = jnp.concatenate([u3, d3])
    ru, rd = go_x(r, 0), go_x(r, 1)
    pu, pd = hook(3, (pu, pd))
    px = go_x(tie(pd, pu), 0)
    qu, qd = hook(4, (qu, qd))
    qx = go_x(tie(qu, qd), 1)
    ru, rd = hook(5, (ru, rd))
    rx = go_x(tie(rd, ru), 0)
    hook(6, px)
    return [p, pu, pd, px, q, qu, qd, qx, r, ru, rd, rx]


def dot(a, b, ca=1, cb=0):
    return lax.dot_general(a, b, (((ca,), (cb,)), ((), ())), preferred_element_type=F32)


def load(pairs, sems):
    copies = [pltpu.make_async_copy(src, dst, sems.at[i]) for i, (src, dst) in enumerate(pairs)]
    for c in copies:
        c.start()
    return copies


def select_kernel(count_any, rows_any, x_any, sel_ref, out_ref, count_ref, rows_ref, x_ref, sems):
    for c in load([(count_any, count_ref), (rows_any, rows_ref), (x_any, x_ref)], sems):
        c.wait()
    lane = lax.broadcasted_iota(jnp.int32, (1, TILE), 1)
    row = lax.broadcasted_iota(jnp.int32, (2 * TILE, TILE), 0)
    for s in range(8):
        listed = jnp.where(lane < count_ref[s], rows_ref[s : s + 1, :], -1)
        sel = jnp.where(row == listed, 1.0, 0.0).astype(BF)
        sel_ref[:, s * TILE : (s + 1) * TILE] = sel
        out_ref[s] = dot(sel, x_ref[...], 0, 0).astype(BF)


def sparse_kernel(rows_any, cols_any, tiles_any, rec_any, out_ref, sum_ref, rows_ref, cols_ref, tiles_ref, rec_ref, total, sems):
    copies = load([(rows_any, rows_ref), (cols_any, cols_ref), (tiles_any, tiles_ref), (rec_any, rec_ref)], sems)
    total[...] = jnp.zeros_like(total)
    for c in copies:
        c.wait()
    for u in range(32):
        at = rows_ref[u] * 8 + cols_ref[u]
        total[at] += tiles_ref[u].astype(F32)
    for r in range(2):
        rows = slice(r * TILE, (r + 1) * TILE)
        for q in range(8):
            high, low = split(total[r * 8 + q])
            out_ref[rows, q * TILE : (q + 1) * TILE] = high
            out_ref[rows, (8 + q) * TILE : (9 + q) * TILE] = low
    half = 8 * TILE
    sum_ref[...] = dot(out_ref[:, :half], rec_ref[...]) + dot(out_ref[:, half:], rec_ref[...])


def split(v):
    high = v.astype(BF)
    return high, (v - high.astype(F32)).astype(BF)


def dense_product(cols_ref, tiles_ref, piece_any, pieces, sems, ready):
    copies = load(list(zip(piece_any, pieces)), sems)
    for c in ready:
        c.wait()
    blk = lax.axis_index("blk")
    x, z = blk // NZ, blk % NZ
    sx, sz = 1 - 2 * (x % 2), 1 - 2 * (z % 2)
    xs = [lax.rem(x + NX + k * sx, NX) * NZ for k in (0, 1, -1, 2)]
    zs = [[lax.rem(z + NZ + k * sz, NZ) for k in part] for part in ((0, 1, -1), (2, -2, 4), (3, -3))]
    sums = [jnp.zeros((TILE, 2 * TILE), F32) for _ in range(2)]
    held = []
    for i, part in enumerate(zs):
        for j, xv in enumerate(xs):
            held += [(xv + zv, 4 * i + j, 2 * TILE * k) for k, zv in enumerate(part)]
    waited = set()
    for n in range(0, len(held), 2):
        pair = held[n : n + 2]
        for _, piece, _ in pair:
            if piece not in waited:
                copies[piece].wait()
                waited.add(piece)
        for r in range(2):
            left = jnp.concatenate([tiles_ref[2 * c + r] for c, _, _ in pair], axis=1)
            right = [
                pieces[p][pl.ds(pl.multiple_of(at + cols_ref[2 * c + r] * TILE, TILE), TILE), :] for c, p, at in pair
            ]
            sums[r] = sums[r] + dot(left, jnp.concatenate(right, axis=0))
    return jnp.concatenate(sums, axis=0)


def forward_kernel(*refs):
    cols_any, tiles_any, s_any, sum_any, w_any, cot_any = refs[:6]
    pieces = refs[6 : 6 + PIECES]
    hidden_ref, grad_ref, back_ref = refs[6 + PIECES : 9 + PIECES]
    cols_ref, tiles_ref, s_ref, sum_ref, w_ref, cot_ref, sems, piece_sems = refs[9 + PIECES : 16 + PIECES + 1]
    ins = [(cols_any, cols_ref), (tiles_any, tiles_ref), (sum_any, sum_ref)]
    copies = load(ins + [(w_any, w_ref), (cot_any, cot_ref), (s_any, s_ref)], sems)
    agg = dense_product(cols_ref, tiles_ref, pieces, refs[-PIECES:], piece_sems, copies[:2])
    for c in copies[2:]:
        c.wait()
    half = 8 * TILE
    high, low = split(agg + sum_ref[...])
    pre = dot(high, w_ref[...]) + dot(low, w_ref[...])
    sig = jax.nn.sigmoid(pre)
    hidden_ref[...] = (pre * sig).astype(BF)
    grad = (cot_ref[...].astype(F32) * sig * (1.0 + pre * (1.0 - sig))).astype(BF)
    grad_ref[...] = grad
    slots = (dot(s_ref[:, :half], grad, 0, 0) + dot(s_ref[:, half:], grad, 0, 0)).astype(BF)
    high, low = split(dot(high, grad, 0, 0) + dot(low, grad, 0, 0))
    for g in range(8):
        back_ref[g, :TILE] = slots[g * TILE : (g + 1) * TILE]
        back_ref[g, TILE : TILE + 32] = high[g * 32 : (g + 1) * 32]
        back_ref[g, TILE + 32 :] = low[g * 32 : (g + 1) * 32]


def backward_kernel(*refs):
    cols_any, tiles_any, sel_any, ret_any, w_any = refs[:5]
    pieces = refs[5 : 5 + PIECES]
    out_ref, cols_ref, tiles_ref, sel_ref, ret_ref, w_ref, sems, piece_sems = refs[5 + PIECES : 13 + PIECES]
    ins = [(cols_any, cols_ref), (tiles_any, tiles_ref), (sel_any, sel_ref)]
    copies = load(ins + [(ret_any, ret_ref), (w_any, w_ref)], sems)
    agg = dense_product(cols_ref, tiles_ref, pieces, refs[-PIECES:], piece_sems, copies[:2])
    for c in copies[2:]:
        c.wait()
    for g in range(8):
        agg += dot(sel_ref[:, g * TILE : (g + 1) * TILE], ret_ref[g, :TILE])
    out_ref[...] = dot(agg.astype(BF), w_ref[...], 1, 1).astype(BF)


HBM = pl.BlockSpec(memory_space=pltpu.HBM)
VMEM = pl.BlockSpec(memory_space=pltpu.VMEM)
DMA = pltpu.SemaphoreType.DMA


def call(kernel, ins, outs, scratch, name, flops, pieces=()):
    many = isinstance(outs, list)
    moved = sum(v.size * v.dtype.itemsize for v in list(ins) + (outs if many else [outs]))
    return pl.pallas_call(
        kernel,
        out_shape=outs,
        in_specs=[HBM] * (len(ins) + len(pieces)),
        out_specs=[VMEM] * len(outs) if many else VMEM,
        scratch_shapes=scratch + [pltpu.VMEM(p.shape, BF) for p in pieces],
        compiler_params=pltpu.CompilerParams(vmem_limit_bytes=VMEM_LIMIT),
        cost_estimate=pl.CostEstimate(flops=flops, bytes_accessed=moved, transcendentals=0),
        name=name,
    )(*ins, *pieces)


def body(
    features,
    weight,
    cotangent,
    dense_tiles,
    dense_cols,
    sparse_tiles,
    sparse_rows,
    sparse_cols,
    send_rows,
    send_counts,
):
    shape = jax.ShapeDtypeStruct
    own = features[0]
    ints, tiles = dense_cols[0, 0], dense_tiles[0, 0]
    square = (256, 256)
    held = []
    for i, part in enumerate(zs):
        for j, xv in enumerate(xs):
            held += [(xv + zv, pieces[4 * i + j], 2 * TILE * k) for k, zv in enumerate(part)]
    for n in range(0, len(held), 2):
        pair = held[n : n + 2]
        for r in range(2):
            left = jnp.concatenate([tiles_ref[2 * c + r] for c, _, _ in pair], axis=1)
            right = [ref[pl.ds(pl.multiple_of(at + cols_ref[2 * c + r] * TILE, TILE), TILE), :] for c, ref, at in pair]
            sums[r] = sums[r] + dot(left, jnp.concatenate(right, axis=0))
    return jnp.concatenate(sums, axis=0)


def forward_kernel(*refs):
    cols_any, tiles_any, s_any, sum_any, w_any, cot_any = refs[:6]
    pieces = refs[6 : 6 + PIECES]
    hidden_ref, grad_ref, back_ref = refs[6 + PIECES : 9 + PIECES]
    cols_ref, tiles_ref, s_ref, sum_ref, w_ref, cot_ref, sems, piece_sems = refs[9 + PIECES : 16 + PIECES + 1]
    ins = [(cols_any, cols_ref), (tiles_any, tiles_ref), (sum_any, sum_ref)]
    copies = load(ins + [(w_any, w_ref), (cot_any, cot_ref), (s_any, s_ref)], sems)
    agg = dense_product(cols_ref, tiles_ref, pieces, refs[-PIECES:], piece_sems, copies[:2])
    for c in copies[2:]:
        c.wait()
    half = 8 * TILE
    high, low = split(agg + sum_ref[...])
    pre = dot(high, w_ref[...]) + dot(low, w_ref[...])
    sig = jax.nn.sigmoid(pre)
    hidden_ref[...] = (pre * sig).astype(BF)
    grad = (cot_ref[...].astype(F32) * sig * (1.0 + pre * (1.0 - sig))).astype(BF)
    grad_ref[...] = grad
    slots = (dot(s_ref[:, :half], grad, 0, 0) + dot(s_ref[:, half:], grad, 0, 0)).astype(BF)
    high, low = split(dot(high, grad, 0, 0) + dot(low, grad, 0, 0))
    for g in range(8):
        back_ref[g, :TILE] = slots[g * TILE : (g + 1) * TILE]
        back_ref[g, TILE : TILE + 32] = high[g * 32 : (g + 1) * 32]
        back_ref[g, TILE + 32 :] = low[g * 32 : (g + 1) * 32]


def backward_kernel(*refs):
    cols_any, tiles_any, sel_any, ret_any, w_any = refs[:5]
    pieces = refs[5 : 5 + PIECES]
    out_ref, cols_ref, tiles_ref, sel_ref, ret_ref, w_ref, sems, piece_sems = refs[5 + PIECES : 13 + PIECES]
    ins = [(cols_any, cols_ref), (tiles_any, tiles_ref), (sel_any, sel_ref)]
    copies = load(ins + [(ret_any, ret_ref), (w_any, w_ref)], sems)
    agg = dense_product(cols_ref, tiles_ref, pieces, refs[-PIECES:], piece_sems, copies[:2])
    for c in copies[2:]:
        c.wait()
    for g in range(8):
        agg += dot(sel_ref[:, g * TILE : (g + 1) * TILE], ret_ref[g, :TILE])
    out_ref[...] = dot(agg.astype(BF), w_ref[...], 1, 1).astype(BF)


HBM = pl.BlockSpec(memory_space=pltpu.HBM)
VMEM = pl.BlockSpec(memory_space=pltpu.VMEM)
DMA = pltpu.SemaphoreType.DMA


def call(kernel, ins, outs, scratch, name, flops, pieces=()):
    many = isinstance(outs, list)
    moved = sum(v.size * v.dtype.itemsize for v in list(ins) + (outs if many else [outs]))
    return pl.pallas_call(
        kernel,
        out_shape=outs,
        in_specs=[HBM] * (len(ins) + len(pieces)),
        out_specs=[VMEM] * len(outs) if many else VMEM,
        scratch_shapes=scratch + [pltpu.VMEM(p.shape, BF) for p in pieces],
        compiler_params=pltpu.CompilerParams(vmem_limit_bytes=VMEM_LIMIT),
        cost_estimate=pl.CostEstimate(flops=flops, bytes_accessed=moved, transcendentals=0),
        name=name,
    )(*ins, *pieces)


def body(
    features,
    weight,
    cotangent,
    dense_tiles,
    dense_cols,
    sparse_tiles,
    sparse_rows,
    sparse_cols,
    send_rows,
    send_counts,
):
    shape = jax.ShapeDtypeStruct
    own = features[0]
    ints, tiles = dense_cols[0, 0], dense_tiles[0, 0]
    square = (256, 256)
    sel, outgoing = call(
        select_kernel,
        [send_counts[0, 0], send_rows[0, 0], own],
        [shape((256, 1024), BF), shape((8, TILE, 256), BF)],
        [pltpu.SMEM((8,), jnp.int32), pltpu.VMEM((8, TILE), jnp.int32), pltpu.VMEM(square, BF), DMA((3,))],
        "select",
        2 * 1024 * 256 * 256,
    )
    received = lax.all_to_all(outgoing, "grp", 0, 0, tiled=True).reshape(1024, 256)
    held = []

    def forward_hook(i, values):
        if i == SELECT_AT:

            held.extend([sel, received])
        if i == 4:
            rec = tie(held[1], values)
            held.extend(
                call(
                    sparse_kernel,
                    [sparse_rows[0, 0], sparse_cols[0, 0], sparse_tiles[0, 0], rec],
                    [shape((256, 2048), BF), shape(square, F32)],
                    [
                        pltpu.SMEM((32,), jnp.int32),
                        pltpu.SMEM((32,), jnp.int32),
                        pltpu.VMEM((32, TILE, TILE), BF),
                        pltpu.VMEM((1024, 256), BF),
                        pltpu.VMEM((16, TILE, TILE), F32),
                        DMA((4,)),
                    ],
                    "sparse",
                    2 * 256 * 2048 * 256,
                )
            )
        return values

    pieces = gather(own, forward_hook)
    sel, _, sparse, sparse_sum = held
    dense_scratch = [pltpu.SMEM((64,), jnp.int32), pltpu.VMEM((64, TILE, TILE), BF)]
    hidden, grad, back = call(
        forward_kernel,
        [ints, tiles, sparse, sparse_sum, weight, cotangent[0]],
        [shape(square, BF), shape(square, BF), shape((8, TILE + 64, 256), BF)],
        dense_scratch
        + [pltpu.VMEM((256, 2048), BF), pltpu.VMEM(square, F32), pltpu.VMEM(square, BF), pltpu.VMEM(square, BF), DMA((6,)), DMA((PIECES,))],
        "forward",
        2 * 256 * 4096 * 256,
        pieces,
    )
    returned = lax.all_to_all(back, "grp", 0, 0, tiled=True)
    part = []

    def add_partner(step, done):
        value = tie(part[0], done)
        part[0] = value + lax.ppermute(value, "blk", [(i, i ^ (1 << step)) for i in range(NX * NZ)])

    def backward_hook(i, values):
        if i == 3:
            part.append(jnp.sum(returned[:, TILE:].astype(F32).reshape(8, 2, 32, 256), axis=(0, 1)))
            add_partner(0, values)
        if i == 4:
            add_partner(1, values)
            add_partner(2, part[0])
        if i == 5:
            add_partner(3, values)
        if i == 6:
            add_partner(4, values)
        return values

    grad_pieces = gather(grad, backward_hook)
    total = part[0] * float(65536) ** -0.5
    grad_weight = lax.all_to_all(jnp.broadcast_to(total[None], (8, 32, 256)), "grp", 0, 0, tiled=True)
    grad_features = call(
        backward_kernel,
        [ints, tiles, sel, returned, weight],
        shape(square, BF),
        dense_scratch + [pltpu.VMEM((256, 1024), BF), pltpu.VMEM((8, TILE + 64, 256), BF), pltpu.VMEM(square, BF), DMA((5,)), DMA((PIECES,))],
        "backward",
        2 * 256 * 4096 * 256,
        grad_pieces,
    )
    return hidden[None], grad_features[None], grad_weight.reshape(256, 256)


def solution(mesh):
    three, four = P("grp", "blk", None), P("grp", "blk", None, None)
    five = P("grp", "blk", None, None, None)
    return jax.shard_map(
        body,
        mesh=mesh,
        in_specs=(three, P(), three, five, three, five, three, three, four, three),
        out_specs=(three, three, P()),
        check_vma=False,
    )
```

```python
import jax
import jax.numpy as jnp
from jax import lax
from jax.experimental import pallas as pl
from jax.experimental.pallas import tpu as pltpu
from jax.sharding import PartitionSpec as P

NX, NZ = 4, 8
TILE = 128
SELECT_AT = 2
BF = jnp.bfloat16
F32 = jnp.float32
VMEM_LIMIT = 58 * 1024 * 1024


def swap_z(kind):
    def partner(z):
        if kind == 0:
            return z ^ 1
        return (z - 1) % NZ if z % 2 == 0 else (z + 1) % NZ

    return [(x * NZ + z, x * NZ + partner(z)) for x in range(NX) for z in range(NZ)]


def swap_x(kind):
    def partner(x):
        if kind == 0:
            return x ^ 1
        return (x - 1) % NX if x % 2 == 0 else (x + 1) % NX

    return [(x * NZ + z, partner(x) * NZ + z) for x in range(NX) for z in range(NZ)]


def go_z(v, kind):
    return lax.ppermute(v, "blk", swap_z(kind))


def go_x(v, kind):
    return lax.ppermute(v, "blk", swap_x(kind))


def tie(values, *others):
    return lax.optimization_barrier((values, others))[0]


def gather(v, hook):
    u1, d1 = go_z(v, 0), go_z(v, 1)
    u1, d1 = hook(0, (u1, d1))
    u2, d2 = go_z(d1, 0), go_z(u1, 1)
    p = jnp.concatenate([v, u1, d1])
    pu, pd = go_x(p, 0), go_x(p, 1)
    u2, d2 = hook(1, (u2, d2))
    u3, d3 = go_z(d2, 0), go_z(u2, 1)
    q = jnp.concatenate([u2, d2])
    qu, qd = go_x(q, 0), go_x(q, 1)
    u3, d3 = hook(2, (u3, d3))
    t = go_z(d3, 0)
    r = jnp.concatenate([u3, d3])
    ru, rd = go_x(r, 0), go_x(r, 1)
    pu, pd = hook(3, (pu, pd))
    px = go_x(tie(pd, pu), 0)
    qu, qd = hook(4, (qu, qd))
    qx = go_x(tie(qu, qd), 1)
    hook(6, [p, pu, pd, q, qu, qd, t])
    t = hook(7, t)
    tu, td = go_x(t, 0), go_x(t, 1)
    ru, rd = hook(5, (ru, rd))
    rx = go_x(tie(rd, ru), 0)
    tu, td = hook(8, (tu, td))
    tx = go_x(tie(tu, td), 1)
    hook(9, (px, tu, td))
    hook(10, (qx, tx))
    hook(11, rx)
    return [p, pu, pd, px, q, qu, qd, qx, r, ru, rd, rx, t, tu, td, tx]


def dot(a, b, ca=1, cb=0):
    return lax.dot_general(a, b, (((ca,), (cb,)), ((), ())), preferred_element_type=F32)


def load(pairs, sems):
    copies = [pltpu.make_async_copy(src, dst, sems.at[i]) for i, (src, dst) in enumerate(pairs)]
    for c in copies:
        c.start()
    return copies


def select_kernel(count_any, rows_any, x_any, sel_ref, out_ref, count_ref, rows_ref, x_ref, sems):
    for c in load([(count_any, count_ref), (rows_any, rows_ref), (x_any, x_ref)], sems):
        c.wait()
    lane = lax.broadcasted_iota(jnp.int32, (1, TILE), 1)
    row = lax.broadcasted_iota(jnp.int32, (2 * TILE, TILE), 0)
    for s in range(8):
        listed = jnp.where(lane < count_ref[s], rows_ref[s : s + 1, :], -1)
        sel = jnp.where(row == listed, 1.0, 0.0).astype(BF)
        sel_ref[:, s * TILE : (s + 1) * TILE] = sel
        out_ref[s] = dot(sel, x_ref[...], 0, 0).astype(BF)


def sparse_kernel(rows_any, cols_any, tiles_any, rec_any, out_ref, sum_ref, rows_ref, cols_ref, tiles_ref, rec_ref, total, sems):
    copies = load([(rows_any, rows_ref), (cols_any, cols_ref), (tiles_any, tiles_ref), (rec_any, rec_ref)], sems)
    total[...] = jnp.zeros_like(total)
    for c in copies:
        c.wait()
    for u in range(32):
        at = rows_ref[u] * 8 + cols_ref[u]
        total[at] += tiles_ref[u].astype(F32)
    for r in range(2):
        rows = slice(r * TILE, (r + 1) * TILE)
        for q in range(8):
            high, low = split(total[r * 8 + q])
            out_ref[rows, q * TILE : (q + 1) * TILE] = high
            out_ref[rows, (8 + q) * TILE : (9 + q) * TILE] = low
    half = 8 * TILE
    sum_ref[...] = dot(out_ref[:, :half], rec_ref[...]) + dot(out_ref[:, half:], rec_ref[...])


def split(v):
    high = v.astype(BF)
    return high, (v - high.astype(F32)).astype(BF)


EARLY = (0, 1, 2, 4, 5, 6, 12)
ALL = tuple(range(16))
LATE = (3, 7, 8, 9, 10, 11, 13, 14, 15)


def dense_product(ids, cols_ref, cols_copy, tiles_any, tiles_ref, tile_sems, piece_any, pieces, piece_sems):
    blk = lax.axis_index("blk")
    x, z = blk // NZ, blk % NZ
    sx, sz = 1 - 2 * (x % 2), 1 - 2 * (z % 2)
    xs = [lax.rem(x + NX + k * sx, NX) * NZ for k in (0, 1, -1, 2)]
    zs = [[lax.rem(z + NZ + k * sz, NZ) for k in part] for part in ((0, 1, -1), (2, -2), (3, -3), (4,))]
    held = []
    for n, piece in enumerate(ids):
        held += [(xs[piece % 4] + zv, n, 2 * TILE * k) for k, zv in enumerate(zs[piece // 4])]
    tiles = load([(tiles_any.at[pl.ds(2 * c, 2)], tiles_ref.at[pl.ds(2 * n, 2)]) for n, (c, _, _) in enumerate(held)], tile_sems)
    copies = load(list(zip(piece_any, pieces)), piece_sems)
    cols_copy.wait()
    sums = [jnp.zeros((TILE, 2 * TILE), F32) for _ in range(2)]
    waited = set()
    for n in range(0, len(held), 2):
        pair = held[n : n + 2]
        tiles[n].wait()
        tiles[n + 1].wait()
        for _, piece, _ in pair:
            if piece not in waited:
                copies[piece].wait()
                waited.add(piece)
        for r in range(2):
            left = jnp.concatenate([tiles_ref[2 * n + r], tiles_ref[2 * n + 2 + r]], axis=1)
            right = [
                pieces[p][pl.ds(pl.multiple_of(at + cols_ref[2 * c + r] * TILE, TILE), TILE), :] for c, p, at in pair
            ]
            sums[r] = sums[r] + dot(left, jnp.concatenate(right, axis=0))
    return jnp.concatenate(sums, axis=0)


def dense_scratch(pieces):
    blocks = sum(p.shape[0] for p in pieces) // (2 * TILE)
    return [pltpu.SMEM((64,), jnp.int32), pltpu.VMEM((2 * blocks, TILE, TILE), BF), DMA((blocks,)), DMA((len(pieces),))]


def early_kernel(*refs):
    n = len(EARLY)
    cols_any, tiles_any = refs[:2]
    out_ref, sems, cols_ref, tiles_ref, tile_sems, piece_sems = refs[2 + n : 8 + n]
    (cols_copy,) = load([(cols_any, cols_ref)], sems)
    out_ref[...] = dense_product(
        EARLY, cols_ref, cols_copy, tiles_any, tiles_ref, tile_sems, refs[2 : 2 + n], refs[-n:], piece_sems
    )


def forward_kernel(*refs):
    n = len(ALL)
    cols_any, tiles_any, s_any, sum_any, w_any, cot_any = refs[:6]
    hidden_ref, grad_ref, back_ref = refs[6 + n : 9 + n]
    s_ref, sum_ref, w_ref, cot_ref, sems, cols_ref, tiles_ref, tile_sems, piece_sems = refs[9 + n : 18 + n]
    ins = [(cols_any, cols_ref), (sum_any, sum_ref), (w_any, w_ref), (cot_any, cot_ref)]
    copies = load(ins + [(s_any, s_ref)], sems)
    agg = dense_product(
        ALL, cols_ref, copies[0], tiles_any, tiles_ref, tile_sems, refs[6 : 6 + n], refs[-n:], piece_sems
    )
    for c in copies[1:]:
        c.wait()
    half = 8 * TILE
    high, low = split(agg + sum_ref[...])
    pre = dot(high, w_ref[...]) + dot(low, w_ref[...])
    sig = jax.nn.sigmoid(pre)
    hidden_ref[...] = (pre * sig).astype(BF)
    grad = (cot_ref[...].astype(F32) * sig * (1.0 + pre * (1.0 - sig))).astype(BF)
    grad_ref[...] = grad
    slots = (dot(s_ref[:, :half], grad, 0, 0) + dot(s_ref[:, half:], grad, 0, 0)).astype(BF)
    high, low = split((dot(high, grad, 0, 0) + dot(low, grad, 0, 0)) * float(65536) ** -0.5)
    for g in range(8):
        back_ref[g, :TILE] = slots[g * TILE : (g + 1) * TILE]
        back_ref[g, TILE : TILE + 32] = high[g * 32 : (g + 1) * 32]
        back_ref[g, TILE + 32 :] = low[g * 32 : (g + 1) * 32]


def backward_kernel(*refs):
    n = len(LATE)
    cols_any, tiles_any, early_any, sel_any, ret_any, w_any = refs[:6]
    out_ref, early_ref, sel_ref, ret_ref, w_ref, sems, cols_ref, tiles_ref, tile_sems, piece_sems = refs[6 + n : 16 + n]
    ins = [(cols_any, cols_ref), (early_any, early_ref), (sel_any, sel_ref), (ret_any.at[:, pl.ds(0, TILE)], ret_ref)]
    copies = load(ins + [(w_any, w_ref)], sems)
    agg = dense_product(
        LATE, cols_ref, copies[0], tiles_any, tiles_ref, tile_sems, refs[6 : 6 + n], refs[-n:], piece_sems
    )
    for c in copies[1:]:
        c.wait()
    agg += early_ref[...]
    for g in range(8):
        agg += dot(sel_ref[:, g * TILE : (g + 1) * TILE], ret_ref[g])
    out_ref[...] = dot(agg.astype(BF), w_ref[...], 1, 1).astype(BF)


HBM = pl.BlockSpec(memory_space=pltpu.HBM)
VMEM = pl.BlockSpec(memory_space=pltpu.VMEM)
DMA = pltpu.SemaphoreType.DMA


def call(kernel, ins, outs, scratch, name, flops, pieces=()):
    many = isinstance(outs, list)
    moved = sum(v.size * v.dtype.itemsize for v in list(ins) + (outs if many else [outs]))
    return pl.pallas_call(
        kernel,
        out_shape=outs,
        in_specs=[HBM] * (len(ins) + len(pieces)),
        out_specs=[VMEM] * len(outs) if many else VMEM,
        scratch_shapes=scratch + [pltpu.VMEM(p.shape, BF) for p in pieces],
        compiler_params=pltpu.CompilerParams(vmem_limit_bytes=VMEM_LIMIT),
        cost_estimate=pl.CostEstimate(flops=flops, bytes_accessed=moved, transcendentals=0),
        name=name,
    )(*ins, *pieces)


def body(
    features,
    weight,
    cotangent,
    dense_tiles,
    dense_cols,
    sparse_tiles,
    sparse_rows,
    sparse_cols,
    send_rows,
    send_counts,
):
    shape = jax.ShapeDtypeStruct
    own = features[0]
    ints, tiles = dense_cols[0, 0], dense_tiles[0, 0]
    square = (256, 256)
    sel, outgoing = call(
        select_kernel,
        [send_counts[0, 0], send_rows[0, 0], own],
        [shape((256, 1024), BF), shape((8, TILE, 256), BF)],
        [pltpu.SMEM((8,), jnp.int32), pltpu.VMEM((8, TILE), jnp.int32), pltpu.VMEM(square, BF), DMA((3,))],
        "select",
        2 * 1024 * 256 * 256,
    )
    received = lax.all_to_all(outgoing, "grp", 0, 0, tiled=True).reshape(1024, 256)
    held = []

    def early(taken):
        scratch = [DMA((1,))] + dense_scratch(taken)
        return call(early_kernel, [ints, tiles], shape(square, F32), scratch, "early", 2 * 256 * 2048 * 256, taken)

    sums = []

    def forward_hook(i, values):
        if i == SELECT_AT:

            held.extend([sel, received])
        if i == 4:
            rec = tie(held[1], values)
            held.extend(
                call(
                    sparse_kernel,
                    [sparse_rows[0, 0], sparse_cols[0, 0], sparse_tiles[0, 0], rec],
                    [shape((256, 2048), BF), shape(square, F32)],
                    [
                        pltpu.SMEM((32,), jnp.int32),
                        pltpu.SMEM((32,), jnp.int32),
                        pltpu.VMEM((32, TILE, TILE), BF),
                        pltpu.VMEM((1024, 256), BF),
                        pltpu.VMEM((16, TILE, TILE), F32),
                        DMA((4,)),
                    ],
                    "sparse",
                    2 * 256 * 2048 * 256,
                )
            )
        return values

    pieces = gather(own, forward_hook)
    sel, _, sparse, sparse_sum = held

    hidden, grad, back = call(
        forward_kernel,
        [ints, tiles, sparse, sparse_sum, weight, cotangent[0]],
        [shape(square, BF), shape(square, BF), shape((8, TILE + 64, 256), BF)],
        [pltpu.VMEM((256, 2048), BF), pltpu.VMEM(square, F32), pltpu.VMEM(square, BF)]
        + [pltpu.VMEM(square, BF), DMA((5,))]
        + dense_scratch(pieces),
        "forward",
        2 * 256 * 4096 * 256,
        pieces,
    )
    returned = lax.all_to_all(back, "grp", 0, 0, tiled=True)
    part = []

    def add_group(groups, *done):
        value = tie(part[-1], *done)
        n = len(groups[0])
        shared = lax.all_to_all(
            jnp.broadcast_to(value[None], (n, 32, 256)), "blk", 0, 0, axis_index_groups=groups, tiled=True
        )
        part.append(jnp.sum(shared, axis=0))

    def backward_hook(i, values):
        if i == 0:
            part.append(jnp.sum(returned[:, TILE:].astype(F32).reshape(8, 2, 32, 256), axis=(0, 1)))
        if i == 3:
            add_group([[x * NZ + z for x in range(NX)] for z in range(NZ)], values)
        if i == 6:
            sums.append(early(values))
        if i == 8:
            add_group([[x * NZ + z for z in range(NZ)] for x in range(NX)], values)
        if i == 9:
            part.append(tie(part[-1], values, sums[0]))
        if i in (10, 11):
            part.append(tie(part[-1], values))
        return values

    grad_pieces = gather(grad, backward_hook)
    shared = jnp.broadcast_to(part[-1][None], (8, 32, 256))
    grad_weight = lax.all_to_all(shared, "grp", 0, 0, tiled=True)
    taken = [grad_pieces[i] for i in LATE]
    grad_features = call(
        backward_kernel,
        [ints, tiles, sums[0], sel, returned, weight],
        shape(square, BF),
        [pltpu.VMEM(square, F32), pltpu.VMEM((256, 1024), BF), pltpu.VMEM((8, TILE, 256), BF), pltpu.VMEM(square, BF)]
        + [DMA((5,))]
        + dense_scratch(taken),
        "backward",
        2 * 256 * 2048 * 256,
        taken,
    )
    return hidden[None], grad_features[None], grad_weight.reshape(256, 256)


def solution(mesh):
    three, four = P("grp", "blk", None), P("grp", "blk", None, None)
    five = P("grp", "blk", None, None, None)
    return jax.shard_map(
        body,
        mesh=mesh,
        in_specs=(three, P(), three, five, three, five, three, three, four, three),
        out_specs=(three, three, P()),
        check_vma=False,
    )
```

```python
import jax
import jax.numpy as jnp
from jax import lax
from jax.experimental import pallas as pl
from jax.experimental.pallas import tpu as pltpu
from jax.sharding import PartitionSpec as P

NX, NZ = 4, 8
TILE = 128
SELECT_AT = 2
BF = jnp.bfloat16
F32 = jnp.float32
VMEM_LIMIT = 58 * 1024 * 1024


def swap_z(kind):
    def partner(z):
        if kind == 0:
            return z ^ 1
        return (z - 1) % NZ if z % 2 == 0 else (z + 1) % NZ

    return [(x * NZ + z, x * NZ + partner(z)) for x in range(NX) for z in range(NZ)]


def swap_x(kind):
    def partner(x):
        if kind == 0:
            return x ^ 1
        return (x - 1) % NX if x % 2 == 0 else (x + 1) % NX

    return [(x * NZ + z, partner(x) * NZ + z) for x in range(NX) for z in range(NZ)]


def go_z(v, kind):
    return lax.ppermute(v, "blk", swap_z(kind))


def go_x(v, kind):
    return lax.ppermute(v, "blk", swap_x(kind))


def tie(values, *others):
    return lax.optimization_barrier((values, others))[0]


def gather(v, hook):
    u1, d1 = go_z(v, 0), go_z(v, 1)
    u1, d1 = hook(0, (u1, d1))
    u2, d2 = go_z(d1, 0), go_z(u1, 1)
    p = jnp.concatenate([v, u1, d1])
    pu, pd = go_x(p, 0), go_x(p, 1)
    u2, d2 = hook(1, (u2, d2))
    u3, d3 = go_z(d2, 0), go_z(u2, 1)
    q = jnp.concatenate([u2, d2])
    qu, qd = go_x(q, 0), go_x(q, 1)
    u3, d3 = hook(2, (u3, d3))
    t = go_z(d3, 0)
    r = jnp.concatenate([u3, d3])
    ru, rd = go_x(r, 0), go_x(r, 1)
    pu, pd = hook(3, (pu, pd))
    px = go_x(tie(pd, pu), 0)
    qu, qd = hook(4, (qu, qd))
    qx = go_x(tie(qu, qd), 1)
    hook(6, [p, pu, pd, q, qu, qd, t])
    t = hook(7, t)
    tu, td = go_x(t, 0), go_x(t, 1)
    ru, rd = hook(5, (ru, rd))
    rx = go_x(tie(rd, ru), 0)
    tu, td = hook(8, (tu, td))
    tx = go_x(tie(tu, td), 1)
    hook(9, (px, tu, td))
    hook(10, (qx, tx))
    hook(11, rx)
    return [p, pu, pd, px, q, qu, qd, qx, r, ru, rd, rx, t, tu, td, tx]


def dot(a, b, ca=1, cb=0):
    return lax.dot_general(a, b, (((ca,), (cb,)), ((), ())), preferred_element_type=F32)


def load(pairs, sems):
    copies = [pltpu.make_async_copy(src, dst, sems.at[i]) for i, (src, dst) in enumerate(pairs)]
    for c in copies:
        c.start()
    return copies


def select_kernel(count_any, rows_any, x_any, sel_ref, out_ref, count_ref, rows_ref, x_ref, sems):
    for c in load([(count_any, count_ref), (rows_any, rows_ref), (x_any, x_ref)], sems):
        c.wait()
    lane = lax.broadcasted_iota(jnp.int32, (1, TILE), 1)
    row = lax.broadcasted_iota(jnp.int32, (2 * TILE, TILE), 0)
    for s in range(8):
        listed = jnp.where(lane < count_ref[s], rows_ref[s : s + 1, :], -1)
        sel = jnp.where(row == listed, 1.0, 0.0).astype(BF)
        sel_ref[:, s * TILE : (s + 1) * TILE] = sel
        out_ref[s] = dot(sel, x_ref[...], 0, 0).astype(BF)


def sparse_kernel(rows_any, cols_any, tiles_any, rec_any, out_ref, sum_ref, rows_ref, cols_ref, tiles_ref, rec_ref, total, sems):
    copies = load([(rows_any, rows_ref), (cols_any, cols_ref), (tiles_any, tiles_ref), (rec_any, rec_ref)], sems)
    total[...] = jnp.zeros_like(total)
    for c in copies:
        c.wait()
    for u in range(32):
        at = rows_ref[u] * 8 + cols_ref[u]
        total[at] += tiles_ref[u].astype(F32)
    for r in range(2):
        rows = slice(r * TILE, (r + 1) * TILE)
        for q in range(8):
            high, low = split(total[r * 8 + q])
            out_ref[rows, q * TILE : (q + 1) * TILE] = high
            out_ref[rows, (8 + q) * TILE : (9 + q) * TILE] = low
    half = 8 * TILE
    sum_ref[...] = dot(out_ref[:, :half], rec_ref[...]) + dot(out_ref[:, half:], rec_ref[...])


def split(v):
    high = v.astype(BF)
    return high, (v - high.astype(F32)).astype(BF)


EARLY = (0, 1, 2, 4, 5, 6, 12)
LATE = (3, 7, 8, 9, 10, 11, 13, 14, 15)


def dense_product(ids, cols_ref, cols_copy, tiles_any, tiles_ref, tile_sems, piece_any, pieces, piece_sems):
    blk = lax.axis_index("blk")
    x, z = blk // NZ, blk % NZ
    sx, sz = 1 - 2 * (x % 2), 1 - 2 * (z % 2)
    xs = [lax.rem(x + NX + k * sx, NX) * NZ for k in (0, 1, -1, 2)]
    zs = [[lax.rem(z + NZ + k * sz, NZ) for k in part] for part in ((0, 1, -1), (2, -2), (3, -3), (4,))]
    held = []
    for n, piece in enumerate(ids):
        held += [(xs[piece % 4] + zv, n, 2 * TILE * k) for k, zv in enumerate(zs[piece // 4])]
    tiles = load([(tiles_any.at[pl.ds(2 * c, 2)], tiles_ref.at[pl.ds(2 * n, 2)]) for n, (c, _, _) in enumerate(held)], tile_sems)
    copies = load(list(zip(piece_any, pieces)), piece_sems)
    cols_copy.wait()
    sums = [jnp.zeros((TILE, 2 * TILE), F32) for _ in range(2)]
    waited = set()
    for n in range(0, len(held), 2):
        pair = held[n : n + 2]
        tiles[n].wait()
        tiles[n + 1].wait()
        for _, piece, _ in pair:
            if piece not in waited:
                copies[piece].wait()
                waited.add(piece)
        for r in range(2):
            left = jnp.concatenate([tiles_ref[2 * n + r], tiles_ref[2 * n + 2 + r]], axis=1)
            right = [
                pieces[p][pl.ds(pl.multiple_of(at + cols_ref[2 * c + r] * TILE, TILE), TILE), :] for c, p, at in pair
            ]
            sums[r] = sums[r] + dot(left, jnp.concatenate(right, axis=0))
    return jnp.concatenate(sums, axis=0)


def dense_scratch(pieces):
    blocks = sum(p.shape[0] for p in pieces) // (2 * TILE)
    return [pltpu.SMEM((64,), jnp.int32), pltpu.VMEM((2 * blocks, TILE, TILE), BF), DMA((blocks,)), DMA((len(pieces),))]


def early_kernel(*refs):
    n = len(EARLY)
    cols_any, tiles_any = refs[:2]
    out_ref, sems, cols_ref, tiles_ref, tile_sems, piece_sems = refs[2 + n : 8 + n]
    (cols_copy,) = load([(cols_any, cols_ref)], sems)
    out_ref[...] = dense_product(
        EARLY, cols_ref, cols_copy, tiles_any, tiles_ref, tile_sems, refs[2 : 2 + n], refs[-n:], piece_sems
    )


def forward_kernel(*refs):
    n = len(LATE)
    cols_any, tiles_any, early_any, s_any, sum_any, w_any, cot_any = refs[:7]
    hidden_ref, grad_ref, back_ref = refs[7 + n : 10 + n]
    early_ref, s_ref, sum_ref, w_ref, cot_ref, sems, cols_ref, tiles_ref, tile_sems, piece_sems = refs[10 + n : 20 + n]
    ins = [(cols_any, cols_ref), (early_any, early_ref), (sum_any, sum_ref), (w_any, w_ref), (cot_any, cot_ref)]
    copies = load(ins + [(s_any, s_ref)], sems)
    agg = dense_product(
        LATE, cols_ref, copies[0], tiles_any, tiles_ref, tile_sems, refs[7 : 7 + n], refs[-n:], piece_sems
    )
    for c in copies[1:]:
        c.wait()
    half = 8 * TILE
    high, low = split(agg + early_ref[...] + sum_ref[...])
    pre = dot(high, w_ref[...]) + dot(low, w_ref[...])
    sig = jax.nn.sigmoid(pre)
    hidden_ref[...] = (pre * sig).astype(BF)
    grad = (cot_ref[...].astype(F32) * sig * (1.0 + pre * (1.0 - sig))).astype(BF)
    grad_ref[...] = grad
    slots = (dot(s_ref[:, :half], grad, 0, 0) + dot(s_ref[:, half:], grad, 0, 0)).astype(BF)
    high, low = split((dot(high, grad, 0, 0) + dot(low, grad, 0, 0)) * float(65536) ** -0.5)
    for g in range(8):
        back_ref[g, :TILE] = slots[g * TILE : (g + 1) * TILE]
        back_ref[g, TILE : TILE + 32] = high[g * 32 : (g + 1) * 32]
        back_ref[g, TILE + 32 :] = low[g * 32 : (g + 1) * 32]


def backward_kernel(*refs):
    n = len(LATE)
    cols_any, tiles_any, early_any, sel_any, ret_any, w_any = refs[:6]
    out_ref, early_ref, sel_ref, ret_ref, w_ref, sems, cols_ref, tiles_ref, tile_sems, piece_sems = refs[6 + n : 16 + n]
    ins = [(cols_any, cols_ref), (early_any, early_ref), (sel_any, sel_ref), (ret_any.at[:, pl.ds(0, TILE)], ret_ref)]
    copies = load(ins + [(w_any, w_ref)], sems)
    agg = dense_product(
        LATE, cols_ref, copies[0], tiles_any, tiles_ref, tile_sems, refs[6 : 6 + n], refs[-n:], piece_sems
    )
    for c in copies[1:]:
        c.wait()
    agg += early_ref[...]
    for g in range(8):
        agg += dot(sel_ref[:, g * TILE : (g + 1) * TILE], ret_ref[g])
    out_ref[...] = dot(agg.astype(BF), w_ref[...], 1, 1).astype(BF)


HBM = pl.BlockSpec(memory_space=pltpu.HBM)
VMEM = pl.BlockSpec(memory_space=pltpu.VMEM)
DMA = pltpu.SemaphoreType.DMA


def call(kernel, ins, outs, scratch, name, flops, pieces=()):
    many = isinstance(outs, list)
    moved = sum(v.size * v.dtype.itemsize for v in list(ins) + (outs if many else [outs]))
    return pl.pallas_call(
        kernel,
        out_shape=outs,
        in_specs=[HBM] * (len(ins) + len(pieces)),
        out_specs=[VMEM] * len(outs) if many else VMEM,
        scratch_shapes=scratch + [pltpu.VMEM(p.shape, BF) for p in pieces],
        compiler_params=pltpu.CompilerParams(vmem_limit_bytes=VMEM_LIMIT),
        cost_estimate=pl.CostEstimate(flops=flops, bytes_accessed=moved, transcendentals=0),
        name=name,
    )(*ins, *pieces)


def body(
    features,
    weight,
    cotangent,
    dense_tiles,
    dense_cols,
    sparse_tiles,
    sparse_rows,
    sparse_cols,
    send_rows,
    send_counts,
):
    shape = jax.ShapeDtypeStruct
    own = features[0]
    ints, tiles = dense_cols[0, 0], dense_tiles[0, 0]
    square = (256, 256)
    sel, outgoing = call(
        select_kernel,
        [send_counts[0, 0], send_rows[0, 0], own],
        [shape((256, 1024), BF), shape((8, TILE, 256), BF)],
        [pltpu.SMEM((8,), jnp.int32), pltpu.VMEM((8, TILE), jnp.int32), pltpu.VMEM(square, BF), DMA((3,))],
        "select",
        2 * 1024 * 256 * 256,
    )
    received = lax.all_to_all(outgoing, "grp", 0, 0, tiled=True).reshape(1024, 256)
    held = []

    def early(taken):
        scratch = [DMA((1,))] + dense_scratch(taken)
        return call(early_kernel, [ints, tiles], shape(square, F32), scratch, "early", 2 * 256 * 2048 * 256, taken)

    sums = []

    def forward_hook(i, values):
        if i == SELECT_AT:

            held.extend([sel, received])
        if i == 6:
            sums.append(early(values))
        if i == 8:
            return tie(values, sums[0])
        if i == 4:
            rec = tie(held[1], values)
            held.extend(
                call(
                    sparse_kernel,
                    [sparse_rows[0, 0], sparse_cols[0, 0], sparse_tiles[0, 0], rec],
                    [shape((256, 2048), BF), shape(square, F32)],
                    [
                        pltpu.SMEM((32,), jnp.int32),
                        pltpu.SMEM((32,), jnp.int32),
                        pltpu.VMEM((32, TILE, TILE), BF),
                        pltpu.VMEM((1024, 256), BF),
                        pltpu.VMEM((16, TILE, TILE), F32),
                        DMA((4,)),
                    ],
                    "sparse",
                    2 * 256 * 2048 * 256,
                )
            )
        return values

    pieces = gather(own, forward_hook)
    sel, _, sparse, sparse_sum = held

    taken = [pieces[i] for i in LATE]
    hidden, grad, back = call(
        forward_kernel,
        [ints, tiles, sums[0], sparse, sparse_sum, weight, cotangent[0]],
        [shape(square, BF), shape(square, BF), shape((8, TILE + 64, 256), BF)],
        [pltpu.VMEM(square, F32), pltpu.VMEM((256, 2048), BF), pltpu.VMEM(square, F32), pltpu.VMEM(square, BF)]
        + [pltpu.VMEM(square, BF), DMA((6,))]
        + dense_scratch(taken),
        "forward",
        2 * 256 * 4096 * 256,
        taken,
    )
    returned = lax.all_to_all(back, "grp", 0, 0, tiled=True)
    part = []

    def add_group(groups, *done):
        value = tie(part[-1], *done)
        n = len(groups[0])
        shared = lax.all_to_all(
            jnp.broadcast_to(value[None], (n, 32, 256)), "blk", 0, 0, axis_index_groups=groups, tiled=True
        )
        part.append(jnp.sum(shared, axis=0))

    def backward_hook(i, values):
        if i == 0:
            part.append(jnp.sum(returned[:, TILE:].astype(F32).reshape(8, 2, 32, 256), axis=(0, 1)))
        if i == 3:
            add_group([[x * NZ + z for x in range(NX)] for z in range(NZ)], values)
        if i == 6:
            sums.append(early(values))
        if i == 8:
            add_group([[x * NZ + z for z in range(NZ)] for x in range(NX)], values)
        if i == 9:
            part.append(tie(part[-1], values, sums[1]))
        if i in (10, 11):
            part.append(tie(part[-1], values))
        return values

    grad_pieces = gather(grad, backward_hook)
    shared = jnp.broadcast_to(part[-1][None], (8, 32, 256))
    grad_weight = lax.all_to_all(shared, "grp", 0, 0, tiled=True)
    taken = [grad_pieces[i] for i in LATE]
    grad_features = call(
        backward_kernel,
        [ints, tiles, sums[1], sel, returned, weight],
        shape(square, BF),
        [pltpu.VMEM(square, F32), pltpu.VMEM((256, 1024), BF), pltpu.VMEM((8, TILE, 256), BF), pltpu.VMEM(square, BF)]
        + [DMA((5,))]
        + dense_scratch(taken),
        "backward",
        2 * 256 * 2048 * 256,
        taken,
    )
    return hidden[None], grad_features[None], grad_weight.reshape(256, 256)


def solution(mesh):
    three, four = P("grp", "blk", None), P("grp", "blk", None, None)
    five = P("grp", "blk", None, None, None)
    return jax.shard_map(
        body,
        mesh=mesh,
        in_specs=(three, P(), three, five, three, five, three, three, four, three),
        out_specs=(three, three, P()),
        check_vma=False,
    )
```
